1024 devices in a mesh: dp: 32 (over z_hi, y, core), section: 4 (over x), mp: 8 (over z_lo).
Axes of the slice: x: 4, y: 4, z: 32 (z_hi: 4, z_lo: 8; z = z_hi * 8 + z_lo), core: 2. Of those that a mesh axis runs over, the one named last changes fastest.
Arguments:
- queries: bfloat16 [4, 64, 128, 4096], P('section', 'dp', None, 'mp'), may hold values from -72 to 72
- latents: bfloat16 [64, 192, 1536], P('dp', None, ('section', 'mp')), may hold values from -6 to 6
- kv_weight: bfloat16 [4, 1536, 2, 4096], P('section', None, None, 'mp'), may hold values from -0.15625 to 0.15625
- token_image: int32 [64, 128], P('dp'), may hold values from 0 to 2
- image_counts: int32 [64], P('dp'), may hold values from 1 to 3, as said below
- out_grad: bfloat16 [4, 64, 128, 4096], P('section', 'dp', None, 'mp'), may hold values from -6 to 6
Outputs:
- attended: bfloat16 [4, 64, 128, 4096], P('section', 'dp', None, 'mp')
- kv_grad: float32 [4, 1536, 2, 4096], P('section', 'dp', None, 'mp')
- latent_grad: float32 [64, 192, 1536], P('dp', None, ('section', 'mp'))
The draws below stay inside these ranges and needn't reach their ends.
Inputs may be any that keep to these rules, and one draw needn't show every extreme that they name: `image_counts`: every value is at most 3, and the first sample has 3 images.
All inputs are finite; a program needn't handle non-finite values.
Results may differ from the reference program's by a relative error of at most 0.022.
Values may be sent and summed in bfloat16 or wider, within the bound.
No kernel may reach another device: no remote copies, remote signals or barrier semaphores. Data moves between devices by JAX's collectives and lax.ppermute only.
A program may use at most 32 MiB of HBM per device.

```python
import jax
import jax.numpy as jnp
from jax import lax

HEADS = 32
HEAD = 128
DV = 1536
LATENTS = 64
IMG = 3
TEXT = 128
SAMPLES_DEV = 2
HQ = 4096
KEYS = 192
LAYERS = 4
SAMPLES = 64
N_DP = 32


def draw_queries(key, part):
    key = jax.random.fold_in(key, 11)
    first_key = jax.random.fold_in(key, 0)
    values = jnp.clip(jax.random.normal(first_key, (LAYERS, SAMPLES, TEXT, HEADS * HEAD), jnp.float32), -6.0, 6.0)
    return values.astype(jnp.bfloat16)


def draw_image_counts(key, part):
    key = jax.random.fold_in(key, 5)
    counts = jax.random.randint(key, (SAMPLES,), 1, IMG + 1).astype(jnp.int32)
    return jnp.where(jnp.arange(SAMPLES) == 0, IMG, counts).astype(jnp.int32)


def set_ends(array, own_key, least, high):
    place = [jax.random.randint(jax.random.fold_in(own_key, axis), (), 0, length) for axis, length in enumerate(array.shape)]
    main_axis = array.shape.index(max(array.shape))
    next_to = place[:main_axis] + [(place[main_axis] + 1) % array.shape[main_axis]] + place[main_axis + 1:]
    return array.at[tuple(place)].set(least).at[tuple(next_to)].set(high)


def shard_levels(stream_key, shape, cuts, least, top_value):
    def one(axis_at, blocks):
        draws = jax.random.uniform(jax.random.fold_in(jax.random.fold_in(stream_key, 6), axis_at), (blocks,), jnp.float32, least / len(cuts), top_value / len(cuts))
        return jnp.repeat(jnp.exp(draws), shape[axis_at] // blocks).reshape((-1,) + (1,) * (len(shape) - axis_at - 1))

    factor_of = one(*cuts[0])
    for cut in cuts[1:]:
        factor_of = factor_of * one(*cut)
    return factor_of


def noise(own_key, dims, scale, bound, shards=(), dtype=jnp.bfloat16):
    values = scale * jax.random.normal(own_key, dims, jnp.float32)
    if shards:
        values = values * shard_levels(own_key, dims, shards, -0.22, 0.18)
    return jnp.clip(values, -bound, bound).astype(dtype)


def setup_inputs(seed: int = 0) -> dict:
    splits = jax.random.split(jax.random.key(seed), 7)
    queries = draw_queries(jax.random.fold_in(splits[6], 71), 0)
    latents = noise(splits[1], (SAMPLES, KEYS, DV), 1.0, 6.0, ((0, 32), (2, 32)))
    kv_weight = noise(splits[2], (LAYERS, DV, 2, HQ), DV ** -0.5, 0.15625, ((0, 4), (3, 8)))
    token_image = set_ends(jax.random.randint(splits[3], (SAMPLES, TEXT), 0, IMG), jax.random.fold_in(splits[3], 1), 0, IMG - 1).astype(jnp.int32)
    image_counts = draw_image_counts(jax.random.fold_in(splits[6], 71), 0)
    out_grad = noise(splits[5], (LAYERS, SAMPLES, TEXT, HQ), 1.0, 6.0, ((0, 4), (1, 32), (3, 8)))
    return dict(queries=queries, latents=latents, kv_weight=kv_weight, token_image=token_image, image_counts=image_counts, out_grad=out_grad)


def attend(query_rows, kv_rounded, token_rows, count_rows, grad_rows):
    samples, text_len, width = query_rows.shape
    key_count = kv_rounded.shape[1]
    scale = HEAD ** -0.5
    query_heads = query_rows.reshape(samples, text_len, -1, HEAD).astype(jnp.float32)
    key_heads = kv_rounded[:, :, 0].reshape(samples, key_count, -1, HEAD).astype(jnp.float32)
    value_heads = kv_rounded[:, :, 1].reshape(samples, key_count, -1, HEAD).astype(jnp.float32)
    grad_heads = grad_rows.reshape(samples, text_len, -1, HEAD).astype(jnp.float32)
    image_of = (jnp.arange(key_count) // LATENTS).astype(jnp.int32)
    allowed = (image_of[None, None, :] == token_rows[:, :, None]) & (image_of[None, None, :] < count_rows[:, None, None])
    allowed = allowed[:, None]
    scores = jnp.einsum("bthe,brhe->bhtr", query_heads, key_heads) * scale
    row_top = jnp.max(jnp.where(allowed, scores, -1e30), axis=-1, keepdims=True)
    expval = jnp.exp(jnp.where(allowed, scores - row_top, -jnp.inf))
    totals = jnp.sum(expval, axis=-1, keepdims=True)
    attn_prob = expval / jnp.where(totals > 0, totals, 1.0)
    prob_bf = attn_prob.astype(jnp.bfloat16).astype(jnp.float32)
    output = jnp.einsum("bhtr,brhe->bthe", prob_bf, value_heads)
    output = output.reshape(samples, text_len, width).astype(jnp.bfloat16)
    dprob = jnp.einsum("bthe,brhe->bhtr", grad_heads, value_heads)
    dscore = attn_prob * (dprob - jnp.sum(dprob * attn_prob, axis=-1, keepdims=True)) * scale
    dscore = dscore.astype(jnp.bfloat16).astype(jnp.float32)
    dkeys = jnp.einsum("bhtr,bthe->brhe", dscore, query_heads)
    dvalues = jnp.einsum("bhtr,bthe->brhe", prob_bf, grad_heads)
    dkv = jnp.stack([dkeys.reshape(samples, key_count, width), dvalues.reshape(samples, key_count, width)], axis=2)
    return output, dkv.astype(jnp.bfloat16)


def reference(queries, latents, kv_weight, token_image, image_counts, out_grad):
    group_lat = latents.reshape(N_DP, SAMPLES_DEV, KEYS, DV)
    group_tok = token_image.reshape(N_DP, SAMPLES_DEV, TEXT)
    group_cnt = image_counts.reshape(N_DP, SAMPLES_DEV)

    def one_layer(layer_args):
        query_layer, weight_layer, grad_layer = layer_args
        weights = weight_layer.reshape(DV, 2 * HQ)
        group_q = query_layer.reshape(N_DP, SAMPLES_DEV, TEXT, HQ)
        group_g = grad_layer.reshape(N_DP, SAMPLES_DEV, TEXT, HQ)

        def one_group(group_args):
            lat_rows, query_rows, grad_rows, token_rows, count_rows = group_args
            flat_lat = lat_rows.reshape(SAMPLES_DEV * KEYS, DV)
            kv_rounded = jnp.dot(flat_lat, weights, preferred_element_type=jnp.float32).astype(jnp.bfloat16)
            kv_rounded = kv_rounded.reshape(SAMPLES_DEV, KEYS, 2, HQ)
            output, dkv = attend(query_rows, kv_rounded, token_rows, count_rows, grad_rows)
            dflat = dkv.reshape(SAMPLES_DEV * KEYS, 2 * HQ)
            lat_term = jnp.dot(dflat, weights.T, preferred_element_type=jnp.float32)
            weight_term = jnp.dot(flat_lat.T, dflat, preferred_element_type=jnp.float32).astype(jnp.bfloat16)
            return output, lat_term.reshape(SAMPLES_DEV, KEYS, DV), weight_term

        outputs, lat_terms, weight_terms = lax.map(one_group, (group_lat, group_q, group_g, group_tok, group_cnt))
        weight_sum = jnp.sum(weight_terms.astype(jnp.float32), axis=0).reshape(DV, 2, HQ)
        return outputs.reshape(SAMPLES, TEXT, HQ), lat_terms.reshape(SAMPLES, KEYS, DV), weight_sum

    attended, lat_layers, kv_grad = lax.map(one_layer, (queries, kv_weight, out_grad))
    latent_grad = jnp.sum(lat_layers, axis=0)
    return attended, kv_grad, latent_grad
```

```python
import jax
import jax.numpy as jnp
from jax import lax
from jax.sharding import Mesh, PartitionSpec as P

HEAD = 128
LATENTS = 64
SIZES = (("zh", 4), ("y", 4), ("core", 2), ("section", 4), ("mp", 8))
AXES = tuple(name for name, _ in SIZES)
SIZE = dict(SIZES)
DP = ("zh", "y", "core")
f32, bf16 = jnp.float32, jnp.bfloat16


def attend(query_rows, kv_rounded, token_rows, count_rows, grad_rows):
    samples, text_len, width = query_rows.shape
    key_count = kv_rounded.shape[1]
    scale = HEAD ** (-0.5)
    query_heads = query_rows.reshape(samples, text_len, -1, HEAD)
    key_heads = kv_rounded[:, :, 0].reshape(samples, key_count, -1, HEAD)
    value_heads = kv_rounded[:, :, 1].reshape(samples, key_count, -1, HEAD)
    grad_heads = grad_rows.reshape(samples, text_len, -1, HEAD)
    image_of = jnp.arange(key_count) // LATENTS
    allowed = (image_of[None, None, :] == token_rows[:, :, None]) & (
        image_of[None, None, :] < count_rows[:, None, None]
    )
    allowed = allowed[:, None]
    scores = (
        jnp.einsum("bthe,brhe->bhtr", query_heads, key_heads, preferred_element_type=jnp.float32)
        * scale
    )
    row_top = jnp.max(jnp.where(allowed, scores, -1e30), axis=-1, keepdims=True)
    expval = jnp.exp(jnp.where(allowed, scores - row_top, -jnp.inf))
    totals = jnp.sum(expval, axis=-1, keepdims=True)
    attn_prob = expval / jnp.where(totals > 0, totals, 1.0)
    prob_bf = attn_prob.astype(jnp.bfloat16)
    output = jnp.einsum("bhtr,brhe->bthe", prob_bf, value_heads, preferred_element_type=jnp.float32)
    output = output.reshape(samples, text_len, width).astype(jnp.bfloat16)
    dprob = jnp.einsum(
        "bthe,brhe->bhtr", grad_heads, value_heads, preferred_element_type=jnp.float32
    )
    dscore = (
        attn_prob * (dprob - jnp.sum(dprob * attn_prob, axis=-1, keepdims=True)) * scale
    ).astype(jnp.bfloat16)
    dkeys = jnp.einsum("bhtr,bthe->brhe", dscore, query_heads, preferred_element_type=jnp.float32)
    dvalues = jnp.einsum("bhtr,bthe->brhe", prob_bf, grad_heads, preferred_element_type=jnp.float32)
    dkv = jnp.stack(
        [dkeys.reshape(samples, key_count, width), dvalues.reshape(samples, key_count, width)],
        axis=2,
    )
    return (output, dkv.astype(jnp.bfloat16))


def shift(x, axis, step):
    n = SIZE[axis]
    return lax.ppermute(x, axis, [(i, (i + step) % n) for i in range(n)])


def swap(x, axis, bit):
    return lax.ppermute(x, axis, [(i, i ^ bit) for i in range(SIZE[axis])])


def pick(x, index, axis=0):
    return lax.dynamic_index_in_dim(x, index, axis, keepdims=False)


def gather_latents(own):
    mp, section = lax.axis_index("mp"), lax.axis_index("section")
    block = own
    for bit in (4, 2, 1):
        other = swap(block, "mp", bit)
        upper = (mp // bit) % 2 == 1
        block = jnp.where(
            upper, jnp.concatenate([other, block]), jnp.concatenate([block, other])
        )
    parts = [block] + [shift(block, "section", k) for k in (1, 2, 3)]
    descending = jnp.stack(parts[::-1] + parts[::-1])
    ordered = lax.dynamic_slice_in_dim(descending, (3 - section) % 4, 4, 0)
    depth, rows = own.shape
    ordered = ordered.reshape(4, 2, 2, 2, depth, rows).transpose(0, 3, 2, 1, 4, 5)
    return ordered.reshape(32 * depth, rows)


def scatter_direct(x, axis):
    n, me = SIZE[axis], lax.axis_index(axis)
    sent = [shift(pick(x, (me + k) % n).astype(bf16), axis, k) for k in range(1, n)]
    total = pick(x, me).astype(f32)
    for part in sent:
        total = total + part.astype(f32)
    return total


def scatter_halving(x):
    mp = lax.axis_index("mp")
    x = x.reshape((2, 2, 2) + x.shape[1:])
    for bit in (1, 2, 4):
        mine = (mp // bit) % 2
        last = {1: 2, 2: 1, 4: 0}[bit]
        x = pick(x, mine, last) + swap(
            pick(x, 1 - mine, last).astype(bf16), "mp", bit
        ).astype(f32)
    return x


def scatter_zh(x):
    me = lax.axis_index("zh")
    half = x.shape[-1] // 2
    far = pick(x, (me + 2) % 4)
    after, before = pick(x, (me + 1) % 4), pick(x, (me + 3) % 4)
    from_after = shift(far[:, :half].astype(bf16), "zh", 3)
    from_before = shift(far[:, half:].astype(bf16), "zh", 1)
    to_before = jnp.concatenate(
        [before[:, :half] + from_after.astype(f32), before[:, half:]], axis=1
    ).astype(bf16)
    to_after = jnp.concatenate(
        [after[:, :half], after[:, half:] + from_before.astype(f32)], axis=1
    ).astype(bf16)
    return pick(x, me) + shift(to_before, "zh", 3).astype(f32) + shift(to_after, "zh", 1).astype(f32)


def body(queries, latents, kv_weight, token_image, image_counts, out_grad):
    samples, key_count, depth = latents.shape
    rows = samples * key_count
    local_features = kv_weight.shape[-1]
    weights = kv_weight.reshape(-1, 2 * local_features)
    width = weights.shape[0]
    lat_t = gather_latents(latents.reshape(rows, depth).T)
    kv_rounded = lax.dot_general(
        lat_t, weights, (((0,), (0,)), ((), ())), preferred_element_type=f32
    ).astype(bf16)
    kv_rounded = kv_rounded.reshape(samples, key_count, 2, local_features)
    attended, dkv = attend(queries[0], kv_rounded, token_image, image_counts, out_grad[0])
    dflat = dkv.reshape(rows, 2 * local_features)

    core = lax.axis_index("core")
    grad_term = jnp.dot(lat_t, dflat, preferred_element_type=f32).astype(bf16)
    grad_term = grad_term.reshape(4, 4, 2, depth, 2 * local_features)
    grad_sum = pick(grad_term, core, 2).astype(f32) + swap(
        pick(grad_term, 1 - core, 2), "core", 1
    ).astype(f32)
    grad_sum = scatter_direct(grad_sum.transpose(1, 0, 2, 3).astype(bf16), "y")
    kv_grad = scatter_zh(grad_sum)

    lat_term = lax.dot_general(
        weights, dflat, (((1,), (1,)), ((), ())), preferred_element_type=f32
    ).astype(bf16)
    lat_sum = scatter_direct(lat_term.reshape(4, 8, depth, rows), "section")
    latent_grad = scatter_halving(lat_sum)
    return (
        attended[None],
        kv_grad.reshape(1, depth, 2, local_features),
        latent_grad.T.reshape(samples, key_count, depth),
    )


def solution(mesh):
    fine = Mesh(mesh.devices.reshape([n for _, n in SIZES]), AXES)
    return jax.shard_map(
        body,
        mesh=fine,
        in_specs=(
            P("section", DP, None, "mp"),
            P(DP, None, ("section", "mp")),
            P("section", None, None, "mp"),
            P(DP, None),
            P(DP),
            P("section", DP, None, "mp"),
        ),
        out_specs=(
            P("section", DP, None, "mp"),
            P("section", DP, None, "mp"),
            P(DP, None, ("section", "mp")),
        ),
        check_vma=False,
    )
```

```python
import jax
import jax.numpy as jnp
from jax import lax
from jax.sharding import Mesh, PartitionSpec as P

HEAD = 128
LATENTS = 64
SIZES = (("zh", 4), ("y", 4), ("core", 2), ("section", 4), ("mp", 8))
AXES = tuple(name for name, _ in SIZES)
SIZE = dict(SIZES)
DP = ("zh", "y", "core")
f32, bf16 = jnp.float32, jnp.bfloat16


def attend(query_rows, kv_rounded, token_rows, count_rows, grad_rows):
    samples, text_len, width = query_rows.shape
    key_count = kv_rounded.shape[1]
    scale = HEAD ** (-0.5)
    query_heads = query_rows.reshape(samples, text_len, -1, HEAD)
    key_heads = kv_rounded[:, :, 0].reshape(samples, key_count, -1, HEAD)
    value_heads = kv_rounded[:, :, 1].reshape(samples, key_count, -1, HEAD)
    grad_heads = grad_rows.reshape(samples, text_len, -1, HEAD)
    image_of = jnp.arange(key_count) // LATENTS
    allowed = (image_of[None, None, :] == token_rows[:, :, None]) & (
        image_of[None, None, :] < count_rows[:, None, None]
    )
    allowed = allowed[:, None]
    scores = (
        jnp.einsum("bthe,brhe->bhtr", query_heads, key_heads, preferred_element_type=jnp.float32)
        * scale
    )
    row_top = jnp.max(jnp.where(allowed, scores, -1e30), axis=-1, keepdims=True)
    expval = jnp.exp(jnp.where(allowed, scores - row_top, -jnp.inf))
    totals = jnp.sum(expval, axis=-1, keepdims=True)
    attn_prob = expval / jnp.where(totals > 0, totals, 1.0)
    prob_bf = attn_prob.astype(jnp.bfloat16)
    output = jnp.einsum("bhtr,brhe->bthe", prob_bf, value_heads, preferred_element_type=jnp.float32)
    output = output.reshape(samples, text_len, width).astype(jnp.bfloat16)
    dprob = jnp.einsum(
        "bthe,brhe->bhtr", grad_heads, value_heads, preferred_element_type=jnp.float32
    )
    dscore = (
        attn_prob * (dprob - jnp.sum(dprob * attn_prob, axis=-1, keepdims=True)) * scale
    ).astype(jnp.bfloat16)
    dkeys = jnp.einsum("bhtr,bthe->brhe", dscore, query_heads, preferred_element_type=jnp.float32)
    dvalues = jnp.einsum("bhtr,bthe->brhe", prob_bf, grad_heads, preferred_element_type=jnp.float32)
    dkv = jnp.stack(
        [dkeys.reshape(samples, key_count, width), dvalues.reshape(samples, key_count, width)],
        axis=2,
    )
    return (output, dkv.astype(jnp.bfloat16))


def swap(x, axis, bit):
    return lax.ppermute(x, axis, [(i, i ^ bit) for i in range(SIZE[axis])])


PARITY = {"y": "core", "section": "core", "zh": "mp"}


def pairing(axis, first):
    odd = lax.axis_index(PARITY[axis]) % 2
    return 1 + 2 * odd if first else 3 - 2 * odd


def paired(x, axis, first):
    axes = tuple(name for name in AXES if name in (axis, PARITY[axis]))
    pairs = []
    for at in range(SIZE[axes[0]] * SIZE[axes[1]]):
        place = dict(zip(axes, divmod(at, SIZE[axes[1]])))
        odd = place[PARITY[axis]] % 2
        place[axis] ^= 1 + 2 * odd if first else 3 - 2 * odd
        pairs.append((at, place[axes[0]] * SIZE[axes[1]] + place[axes[1]]))
    return lax.ppermute(x, axes, pairs)


def pick(x, index, axis=0):
    return lax.dynamic_index_in_dim(x, index, axis, keepdims=False)


def gather_latents(own):
    mp, section = lax.axis_index("mp"), lax.axis_index("section")
    block = own
    for bit in (4, 2, 1):
        other = swap(block, "mp", bit)
        upper = (mp // bit) % 2 == 1
        block = jnp.where(
            upper, jnp.concatenate([other, block]), jnp.concatenate([block, other])
        )
    second = paired(block, "section", False)
    pair = jnp.stack([block, second])
    far = paired(pair, "section", True)
    parts = jnp.concatenate([pair, far])
    a = pairing("section", True)
    depth, rows = own.shape
    ordered = []
    for s in range(4):
        x = s ^ section
        place = jnp.where(x == 0, 0, jnp.where(x == 2, 3, jnp.where(x == a, 2, 1)))
        ordered.append(pick(parts, place))
    ordered = jnp.stack(ordered).reshape(4, 2, 2, 2, depth, rows).transpose(0, 3, 2, 1, 4, 5)
    return ordered.reshape(32 * depth, rows)


def halve_first(x, axis):
    me, a, b = lax.axis_index(axis), pairing(axis, True), pairing(axis, False)
    send = jnp.stack([pick(x, me ^ a), pick(x, me ^ 2)]).astype(bf16)
    got = paired(send, axis, True).astype(f32)
    return pick(x, me).astype(f32) + got[0], pick(x, me ^ b).astype(f32) + got[1]


def halve_second(mine, other, axis):
    return mine + paired(other.astype(bf16), axis, False).astype(f32)


def halve_mp(x, bit):
    mine = (lax.axis_index("mp") // bit) % 2
    return pick(x, mine).astype(f32) + swap(pick(x, 1 - mine).astype(bf16), "mp", bit).astype(f32)


def body(queries, latents, kv_weight, token_image, image_counts, out_grad):
    samples, key_count, depth = latents.shape
    rows = samples * key_count
    local_features = kv_weight.shape[-1]
    weights = kv_weight.reshape(-1, 2 * local_features)
    width = weights.shape[0]
    lat_t = gather_latents(latents.reshape(rows, depth).T)
    kv_rounded = lax.dot_general(
        lat_t, weights, (((0,), (0,)), ((), ())), preferred_element_type=f32
    ).astype(bf16)
    kv_rounded = kv_rounded.reshape(samples, key_count, 2, local_features)
    attended, dkv = attend(queries[0], kv_rounded, token_image, image_counts, out_grad[0])
    dflat = dkv.reshape(rows, 2 * local_features)

    core = lax.axis_index("core")
    grad_term = jnp.dot(lat_t, dflat, preferred_element_type=f32).astype(bf16)
    grad_term = grad_term.reshape(4, 4, 2, depth, 2 * local_features).transpose(2, 1, 0, 3, 4)
    lat_term = lax.dot_general(
        weights, dflat, (((1,), (1,)), ((), ())), preferred_element_type=f32
    ).astype(bf16)
    lat_term = lat_term.reshape(4, 2, 2, 2, depth, rows).transpose(0, 3, 2, 1, 4, 5)

    grad_sum = pick(grad_term, core).astype(f32) + swap(
        pick(grad_term, 1 - core), "core", 1
    ).astype(f32)
    lat_mine, lat_other = halve_first(lat_term, "section")
    grad_sum, lat_mine, lat_other = lax.optimization_barrier((grad_sum, lat_mine, lat_other))
    mine, other = halve_first(grad_sum, "y")
    lat_sum = halve_second(lat_mine, lat_other, "section")
    mine, other, lat_sum = lax.optimization_barrier((mine, other, lat_sum))
    grad_sum = halve_second(mine, other, "y")
    lat_sum = halve_mp(lat_sum, 1)
    grad_sum, lat_sum = lax.optimization_barrier((grad_sum, lat_sum))
    mine, other = halve_first(grad_sum, "zh")
    lat_sum = halve_mp(lat_sum, 2)
    lat_sum = halve_mp(lat_sum, 4)
    kv_grad = halve_second(mine, other, "zh")
    latent_grad = lat_sum
    return (
        attended[None],
        kv_grad.reshape(1, depth, 2, local_features),
        latent_grad.T.reshape(samples, key_count, depth),
    )


def solution(mesh):
    fine = Mesh(mesh.devices.reshape([n for _, n in SIZES]), AXES)
    return jax.shard_map(
        body,
        mesh=fine,
        in_specs=(
            P("section", DP, None, "mp"),
            P(DP, None, ("section", "mp")),
            P("section", None, None, "mp"),
            P(DP, None),
            P(DP),
            P("section", DP, None, "mp"),
        ),
        out_specs=(
            P("section", DP, None, "mp"),
            P("section", DP, None, "mp"),
            P(DP, None, ("section", "mp")),
        ),
        check_vma=False,
    )
```

```python
import functools

import jax
import jax.numpy as jnp
from jax import lax
from jax.experimental import pallas as pl
from jax.experimental.pallas import tpu as pltpu
from jax.sharding import Mesh, PartitionSpec as P

HEAD = 128
LATENTS = 64
SIZES = (("zh", 4), ("y", 4), ("core", 2), ("section", 4), ("mp", 8))
AXES = tuple(name for name, _ in SIZES)
SIZE = dict(SIZES)
DP = ("zh", "y", "core")
f32, bf16 = jnp.float32, jnp.bfloat16
VMEM = pl.BlockSpec(memory_space=pltpu.VMEM)
SMEM = pl.BlockSpec(memory_space=pltpu.SMEM)
TRANS_A = (((0,), (0,)), ((), ()))
TRANS_B = (((1,), (1,)), ((), ()))


def dot(a, b, dims=(((1,), (0,)), ((), ()))):
    return lax.dot_general(a, b, dims, preferred_element_type=f32)


PARITY = {"y": "core", "section": "core", "zh": "mp"}


def relative(axis):
    me, odd = lax.axis_index(axis), lax.axis_index(PARITY[axis]) % 2
    return [me, me ^ (3 - 2 * odd), me ^ (1 + 2 * odd), me ^ 2]


def paired(x, axis, first):
    axes = tuple(name for name in AXES if name in (axis, PARITY[axis]))
    pairs = []
    for at in range(SIZE[axes[0]] * SIZE[axes[1]]):
        place = dict(zip(axes, divmod(at, SIZE[axes[1]])))
        odd = place[PARITY[axis]] % 2
        place[axis] ^= 1 + 2 * odd if first else 3 - 2 * odd
        pairs.append((at, place[axes[0]] * SIZE[axes[1]] + place[axes[1]]))
    return lax.ppermute(x, axes, pairs)


def swap(x, axis, bit):
    return lax.ppermute(x, axis, [(i, i ^ bit) for i in range(SIZE[axis])])


def gather_latents(own):
    block = own
    for axis in ("mp", "section"):
        copies = jnp.broadcast_to(block, (SIZE[axis],) + block.shape)
        block = lax.all_to_all(copies, axis, 0, 0, tiled=True)
        block = block.reshape((-1,) + block.shape[2:])
    return block


def attend_kernel(keys, counts, lat, weight, query, grad, token, attended, dflat, kv):
    samples, _, width = query.shape
    scale = HEAD ** (-0.5)
    kv[...] = dot(lat[...], weight[...], TRANS_A).astype(bf16)
    image_of = lax.broadcasted_iota(jnp.int32, (keys, query.shape[1]), 0) // LATENTS
    for b in range(samples):
        rows = slice(b * keys, (b + 1) * keys)
        allowed = (image_of == token[b]) & (image_of < counts[b])
        for h in range(width // HEAD):
            low = slice(h * HEAD, (h + 1) * HEAD)
            high = slice(width + h * HEAD, width + (h + 1) * HEAD)
            k, v, q, g = kv[rows, low], kv[rows, high], query[b, :, low], grad[b, :, low]
            scores = dot(k, q, TRANS_B) * scale
            top = jnp.max(jnp.where(allowed, scores, -1e30), axis=0, keepdims=True)
            expval = jnp.where(allowed, jnp.exp(scores - top), 0.0)
            total = jnp.sum(expval, axis=0, keepdims=True)
            prob = expval / jnp.where(total > 0, total, 1.0)
            prob_bf = prob.astype(bf16)
            attended[b, :, low] = dot(prob_bf, v, TRANS_A).astype(bf16)
            dprob = dot(v, g, TRANS_B)
            dscore = prob * (dprob - jnp.sum(dprob * prob, axis=0, keepdims=True)) * scale
            dflat[rows, low] = dot(dscore.astype(bf16), q).astype(bf16)
            dflat[rows, high] = dot(prob_bf, g).astype(bf16)


def latent_kernel(depth, order, place, weight, dflat, out):
    chunk = out.shape[1]
    for i in range(out.shape[0]):
        start = pl.multiple_of(order[i] * chunk, 128)
        term = dot(weight[pl.ds(start, chunk), :], dflat[...], TRANS_B).astype(out.dtype)
        for m in range(chunk // depth):
            at = pl.multiple_of(place[m] * depth, 16)
            out[i, pl.ds(at, depth), :] = term[m * depth : (m + 1) * depth]


def weight_kernel(depth, blocks, lat, dflat, out, picked):
    for i in range(picked.shape[0] // depth):
        start = pl.multiple_of(blocks[i] * depth, 16)
        picked[i * depth : (i + 1) * depth, :] = lat[pl.ds(start, depth), :]
    out[...] = dot(picked[...], dflat[...]).astype(out.dtype)


def call(kernel, specs, shapes, scratch, flops, *args):
    size = sum(a.size * a.dtype.itemsize for a in args)
    return pl.pallas_call(
        kernel,
        out_shape=shapes,
        in_specs=specs,
        out_specs=jax.tree.map(lambda _: VMEM, shapes),
        scratch_shapes=scratch,
        compiler_params=pltpu.CompilerParams(vmem_limit_bytes=40 << 20),
        cost_estimate=pl.CostEstimate(flops=flops, bytes_accessed=size, transcendentals=0),
    )(*args)


def body(queries, latents, kv_weight, token_image, image_counts, out_grad):
    samples, keys, depth = latents.shape
    rows = samples * keys
    _, width, _, local = kv_weight.shape
    weight = kv_weight.reshape(width, 2 * local)
    core, mp = lax.axis_index("core"), lax.axis_index("mp")
    lat = gather_latents(latents.reshape(rows, depth).T)

    attended, dflat = call(
        functools.partial(attend_kernel, keys),
        [SMEM] + [VMEM] * 5,
        (
            jax.ShapeDtypeStruct(queries.shape[1:], bf16),
            jax.ShapeDtypeStruct((rows, 2 * local), bf16),
        ),
        [pltpu.VMEM((rows, 2 * local), bf16)],
        2 * rows * width * 2 * local,
        image_counts,
        lat,
        weight,
        queries[0],
        out_grad[0],
        token_image.reshape(samples, 1, -1),
    )

    to = jnp.arange(8, dtype=jnp.int32) ^ mp
    place = (to % 2) * 4 + (to // 2 % 2) * 2 + to // 4
    order = jnp.stack(relative("section")).astype(jnp.int32)

    def latent_terms(sections, dtype):
        return call(
            functools.partial(latent_kernel, depth),
            [SMEM, SMEM, VMEM, VMEM],
            jax.ShapeDtypeStruct((2, width // 4, rows), dtype),
            [],
            width * rows * 2 * local,
            sections,
            place,
            weight,
            dflat,
        )

    def weight_terms(at_core, ys, dtype, dflat):
        zs = jnp.stack(relative("zh"))
        blocks = (zs[None, :] * 8 + jnp.stack(ys)[:, None] * 2 + at_core).reshape(-1)
        return call(
            functools.partial(weight_kernel, depth),
            [SMEM, VMEM, VMEM],
            jax.ShapeDtypeStruct((width // 2, 2 * local), dtype),
            [pltpu.VMEM((width // 2, rows), bf16)],
            width * rows * 2 * local,
            blocks.astype(jnp.int32),
            lat,
            dflat,
        ).reshape(4, 4, depth, 2 * local)

    mine, second, first, both = relative("y")
    lat_send = latent_terms(order[2:], bf16)
    lat_send, dflat_next = lax.optimization_barrier((lat_send, dflat))
    grad_send = weight_terms(1 - core, [mine, first, second, both], bf16, dflat_next)
    lat_keep = latent_terms(order[:2], f32)
    grad_keep = weight_terms(core, [mine, second, first, both], f32, dflat)

    grad = grad_keep + swap(grad_send, "core", 1).astype(f32)
    lat_sum = lat_keep + paired(lat_send, "section", True).astype(f32)
    grad, lat_sum = lax.optimization_barrier((grad, lat_sum))

    grad = grad[:2] + paired(grad[2:].astype(bf16), "y", True).astype(f32)
    lat_sum = lat_sum[0] + paired(lat_sum[1].astype(bf16), "section", False).astype(f32)
    grad, lat_sum = lax.optimization_barrier((grad, lat_sum))

    grad = grad[0] + paired(grad[1].astype(bf16), "y", False).astype(f32)
    lat_sum = lat_sum.reshape(8, depth, rows)
    lat_sum = lat_sum[:4] + swap(lat_sum[4:].astype(bf16), "mp", 1).astype(f32)
    grad, lat_sum = lax.optimization_barrier((grad, lat_sum))

    grad = grad[:2] + paired(grad[2:].astype(bf16), "zh", True).astype(f32)
    lat_sum = lat_sum[:2] + swap(lat_sum[2:].astype(bf16), "mp", 2).astype(f32)
    lat_sum = lat_sum[0] + swap(lat_sum[1].astype(bf16), "mp", 4).astype(f32)
    kv_grad = grad[0] + paired(grad[1].astype(bf16), "zh", False).astype(f32)
    return (
        attended[None],
        kv_grad.reshape(1, depth, 2, local),
        lat_sum.T.reshape(samples, keys, depth),
    )


def solution(mesh):
    fine = Mesh(mesh.devices.reshape([n for _, n in SIZES]), AXES)
    return jax.shard_map(
        body,
        mesh=fine,
        in_specs=(
            P("section", DP, None, "mp"),
            P(DP, None, ("section", "mp")),
            P("section", None, None, "mp"),
            P(DP, None),
            P(DP),
            P("section", DP, None, "mp"),
        ),
        out_specs=(
            P("section", DP, None, "mp"),
            P("section", DP, None, "mp"),
            P(DP, None, ("section", "mp")),
        ),
        check_vma=False,
    )
```

```python
import functools

import jax
import jax.numpy as jnp
from jax import lax
from jax.experimental import pallas as pl
from jax.experimental.pallas import tpu as pltpu
from jax.sharding import Mesh, PartitionSpec as P

HEAD = 128
LATENTS = 64
SIZES = (("zh", 4), ("y", 4), ("core", 2), ("section", 4), ("mp", 8))
AXES = tuple(name for name, _ in SIZES)
SIZE = dict(SIZES)
DP = ("zh", "y", "core")
f32, bf16 = jnp.float32, jnp.bfloat16
VMEM = pl.BlockSpec(memory_space=pltpu.VMEM)
SMEM = pl.BlockSpec(memory_space=pltpu.SMEM)
TRANS_A = (((0,), (0,)), ((), ()))
TRANS_B = (((1,), (1,)), ((), ()))


def dot(a, b, dims=(((1,), (0,)), ((), ()))):
    return lax.dot_general(a, b, dims, preferred_element_type=f32)


PARITY = {"y": "core", "section": "core", "zh": "mp"}


def relative(axis):
    me, odd = lax.axis_index(axis), lax.axis_index(PARITY[axis]) % 2
    return [me, me ^ (3 - 2 * odd), me ^ (1 + 2 * odd), me ^ 2]


def paired(x, axis, first):
    axes = tuple(name for name in AXES if name in (axis, PARITY[axis]))
    pairs = []
    for at in range(SIZE[axes[0]] * SIZE[axes[1]]):
        place = dict(zip(axes, divmod(at, SIZE[axes[1]])))
        odd = place[PARITY[axis]] % 2
        place[axis] ^= 1 + 2 * odd if first else 3 - 2 * odd
        pairs.append((at, place[axes[0]] * SIZE[axes[1]] + place[axes[1]]))
    return lax.ppermute(x, axes, pairs)


def swap(x, axis, bit):
    return lax.ppermute(x, axis, [(i, i ^ bit) for i in range(SIZE[axis])])


def gather_latents(own):
    block = own
    for axis in ("mp", "section"):
        copies = jnp.broadcast_to(block, (SIZE[axis],) + block.shape)
        block = lax.all_to_all(copies, axis, 0, 0, tiled=True)
        block = block.reshape((-1,) + block.shape[2:])
    return block


def attend_kernel(keys, counts, lat, weight, query, grad, token, attended, dflat, kv):
    samples, _, width = query.shape
    scale = HEAD ** (-0.5)
    kv[...] = dot(lat[...], weight[...], TRANS_A).astype(bf16)
    image_of = lax.broadcasted_iota(jnp.int32, (keys, query.shape[1]), 0) // LATENTS
    for b in range(samples):
        rows = slice(b * keys, (b + 1) * keys)
        allowed = (image_of == token[b]) & (image_of < counts[b])
        for h in range(width // HEAD):
            low = slice(h * HEAD, (h + 1) * HEAD)
            high = slice(width + h * HEAD, width + (h + 1) * HEAD)
            k, v, q, g = kv[rows, low], kv[rows, high], query[b, :, low], grad[b, :, low]
            scores = dot(k, q, TRANS_B) * scale
            top = jnp.max(jnp.where(allowed, scores, -1e30), axis=0, keepdims=True)
            expval = jnp.where(allowed, jnp.exp(scores - top), 0.0)
            total = jnp.sum(expval, axis=0, keepdims=True)
            prob = expval / jnp.where(total > 0, total, 1.0)
            prob_bf = prob.astype(bf16)
            attended[b, :, low] = dot(prob_bf, v, TRANS_A).astype(bf16)
            dprob = dot(v, g, TRANS_B)
            dscore = prob * (dprob - jnp.sum(dprob * prob, axis=0, keepdims=True)) * scale
            dflat[rows, low] = dot(dscore.astype(bf16), q).astype(bf16)
            dflat[rows, high] = dot(prob_bf, g).astype(bf16)


def latent_kernel(weight, dflat, after, out):
    out[...] = dot(weight[...], dflat[...], TRANS_B).astype(bf16)


def pick_blocks(depth, blocks, lat, picked):
    for i in range(picked.shape[0] // depth):
        start = pl.multiple_of(blocks[i] * depth, 16)
        picked[i * depth : (i + 1) * depth, :] = lat[pl.ds(start, depth), :]


def send_kernel(depth, blocks, lat, dflat, out, picked):
    pick_blocks(depth, blocks, lat, picked)
    out[...] = dot(picked[...], dflat[...]).astype(bf16)


def keep_kernel(depth, blocks, lat, dflat, other, keep, send, picked):
    pick_blocks(depth, blocks, lat, picked)
    half = keep.shape[0]
    keep[...] = dot(picked[:half], dflat[...]) + other[:half].astype(f32)
    send[...] = (dot(picked[half:], dflat[...]) + other[half:].astype(f32)).astype(bf16)


def sum_kernel(parts, after, out):
    total = parts[0].astype(f32)
    for i in range(1, parts.shape[0]):
        total += parts[i].astype(f32)
    out[...] = total.astype(bf16)


def call(kernel, specs, shapes, scratch, flops, *args):
    size = sum(a.size * a.dtype.itemsize for a in args)
    return pl.pallas_call(
        kernel,
        out_shape=shapes,
        in_specs=specs,
        out_specs=jax.tree.map(lambda _: VMEM, shapes),
        scratch_shapes=scratch,
        compiler_params=pltpu.CompilerParams(vmem_limit_bytes=16 << 20),
        cost_estimate=pl.CostEstimate(flops=flops, bytes_accessed=size, transcendentals=0),
    )(*args)


def body(queries, latents, kv_weight, token_image, image_counts, out_grad):
    samples, keys, depth = latents.shape
    rows = samples * keys
    _, width, _, local = kv_weight.shape
    weight = kv_weight.reshape(width, 2 * local)
    core = lax.axis_index("core")
    lat = gather_latents(latents.reshape(rows, depth).T)

    attended, dflat = call(
        functools.partial(attend_kernel, keys),
        [SMEM] + [VMEM] * 5,
        (
            jax.ShapeDtypeStruct(queries.shape[1:], bf16),
            jax.ShapeDtypeStruct((rows, 2 * local), bf16),
        ),
        [pltpu.VMEM((rows, 2 * local), bf16)],
        2 * rows * width * 2 * local,
        image_counts,
        lat,
        weight,
        queries[0],
        out_grad[0],
        token_image.reshape(samples, 1, -1),
    )

    half, cols = width // 4, 2 * local
    zs = jnp.stack(relative("zh"))

    def blocks(at_core, ys):
        return (zs[None, :] * 8 + jnp.stack(ys)[:, None] * 2 + at_core).reshape(-1).astype(jnp.int32)

    mine, second, first, both = relative("y")
    picked = [pltpu.VMEM((2 * half, rows), bf16)]
    grad_send = call(
        functools.partial(send_kernel, depth),
        [SMEM, VMEM, VMEM],
        jax.ShapeDtypeStruct((2 * half, cols), bf16),
        picked,
        width * rows * cols,
        blocks(1 - core, [mine, first, second, both]),
        lat,
        dflat,
    )
    lat_term = call(
        latent_kernel,
        [VMEM, VMEM, pl.BlockSpec(memory_space=pl.ANY)],
        jax.ShapeDtypeStruct((width, rows), bf16),
        [],
        2 * width * rows * cols,
        weight,
        dflat,
        grad_send,
    )
    keep, send = call(
        functools.partial(keep_kernel, depth),
        [SMEM, VMEM, VMEM, VMEM],
        (jax.ShapeDtypeStruct((half, cols), f32), jax.ShapeDtypeStruct((half, cols), bf16)),
        picked,
        width * rows * cols,
        blocks(core, [mine, second, first, both]),
        lat,
        dflat,
        swap(grad_send, "core", 1),
    )

    lat_parts = lax.all_to_all(lat_term.reshape(4, half, rows), "section", 0, 0, tiled=True)
    lat_sum = call(
        sum_kernel,
        [VMEM, pl.BlockSpec(memory_space=pl.ANY)],
        jax.ShapeDtypeStruct((half, rows), bf16),
        [],
        4 * half * rows,
        lat_parts,
        send,
    )
    lat_parts = lax.all_to_all(lat_sum.reshape(8, depth, rows), "mp", 0, 0, tiled=True)

    grad = (keep + paired(send, "y", True).astype(f32)).reshape(2, -1, cols)
    grad = grad[0] + paired(grad[1].astype(bf16), "y", False).astype(f32)
    grad = grad.reshape(2, -1, cols)
    grad = grad[0] + paired(grad[1].astype(bf16), "zh", True).astype(f32)
    lat_sum = jnp.sum(lat_parts.astype(f32), axis=0)
    grad, lat_sum = lax.optimization_barrier((grad, lat_sum))
    grad = grad.reshape(2, -1, cols)
    kv_grad = grad[0] + paired(grad[1].astype(bf16), "zh", False).astype(f32)
    return (
        attended[None],
        kv_grad.reshape(1, depth, 2, local),
        lat_sum.T.reshape(samples, keys, depth),
    )


def solution(mesh):
    fine = Mesh(mesh.devices.reshape([n for _, n in SIZES]), AXES)
    return jax.shard_map(
        body,
        mesh=fine,
        in_specs=(
            P("section", DP, None, "mp"),
            P(DP, None, ("section", "mp")),
            P("section", None, None, "mp"),
            P(DP, None),
            P(DP),
            P("section", DP, None, "mp"),
        ),
        out_specs=(
            P("section", DP, None, "mp"),
            P("section", DP, None, "mp"),
            P(DP, None, ("section", "mp")),
        ),
        check_vma=False,
    )
```

```python
import functools

import jax
import jax.numpy as jnp
from jax import lax
from jax.experimental import pallas as pl
from jax.experimental.pallas import tpu as pltpu
from jax.sharding import Mesh, PartitionSpec as P

HEAD = 128
LATENTS = 64
SIZES = (("zh", 4), ("y", 4), ("core", 2), ("section", 4), ("mp", 8))
AXES = tuple(name for name, _ in SIZES)
SIZE = dict(SIZES)
DP = ("zh", "y", "core")
f32, bf16 = jnp.float32, jnp.bfloat16
VMEM = pl.BlockSpec(memory_space=pltpu.VMEM)
SMEM = pl.BlockSpec(memory_space=pltpu.SMEM)
TRANS_A = (((0,), (0,)), ((), ()))
TRANS_B = (((1,), (1,)), ((), ()))


def dot(a, b, dims=(((1,), (0,)), ((), ()))):
    return lax.dot_general(a, b, dims, preferred_element_type=f32)


PARITY = {"y": "core", "section": "core", "zh": "mp"}


def relative(axis):
    me, odd = lax.axis_index(axis), lax.axis_index(PARITY[axis]) % 2
    return [me, me ^ (3 - 2 * odd), me ^ (1 + 2 * odd), me ^ 2]


def paired(x, axis, first):
    axes = tuple(name for name in AXES if name in (axis, PARITY[axis]))
    pairs = []
    for at in range(SIZE[axes[0]] * SIZE[axes[1]]):
        place = dict(zip(axes, divmod(at, SIZE[axes[1]])))
        odd = place[PARITY[axis]] % 2
        place[axis] ^= 1 + 2 * odd if first else 3 - 2 * odd
        pairs.append((at, place[axes[0]] * SIZE[axes[1]] + place[axes[1]]))
    return lax.ppermute(x, axes, pairs)


def swap(x, axis, bit):
    return lax.ppermute(x, axis, [(i, i ^ bit) for i in range(SIZE[axis])])


def gather_latents(own):
    block = own
    for axis in ("mp", "section"):
        copies = jnp.broadcast_to(block, (SIZE[axis],) + block.shape)
        block = lax.all_to_all(copies, axis, 0, 0, tiled=True)
        block = block.reshape((-1,) + block.shape[2:])
    return block


def pick_blocks(depth, blocks, lat, picked):
    for i in range(picked.shape[0] // depth):
        start = pl.multiple_of(blocks[i] * depth, 16)
        picked[i * depth : (i + 1) * depth, :] = lat[pl.ds(start, depth), :]


def main_kernel(
    keys, depth, counts, blocks, lat, weight, query, grad, token, attended, dflat, sent, lat_term, kv, picked
):
    samples, _, width = query.shape
    scale = HEAD ** (-0.5)
    kv[...] = dot(lat[...], weight[...], TRANS_A).astype(bf16)
    image_of = lax.broadcasted_iota(jnp.int32, (keys, query.shape[1]), 0) // LATENTS
    for b in range(samples):
        rows = slice(b * keys, (b + 1) * keys)
        allowed = (image_of == token[b]) & (image_of < counts[b])
        for h in range(width // HEAD):
            low = slice(h * HEAD, (h + 1) * HEAD)
            high = slice(width + h * HEAD, width + (h + 1) * HEAD)
            k, v, q, g = kv[rows, low], kv[rows, high], query[b, :, low], grad[b, :, low]
            scores = dot(k, q, TRANS_B) * scale
            top = jnp.max(jnp.where(allowed, scores, -1e30), axis=0, keepdims=True)
            expval = jnp.where(allowed, jnp.exp(scores - top), 0.0)
            total = jnp.sum(expval, axis=0, keepdims=True)
            prob = expval / jnp.where(total > 0, total, 1.0)
            prob_bf = prob.astype(bf16)
            attended[b, :, low] = dot(prob_bf, v, TRANS_A).astype(bf16)
            dprob = dot(v, g, TRANS_B)
            dscore = prob * (dprob - jnp.sum(dprob * prob, axis=0, keepdims=True)) * scale
            dflat[rows, low] = dot(dscore.astype(bf16), q).astype(bf16)
            dflat[rows, high] = dot(prob_bf, g).astype(bf16)
    pick_blocks(depth, blocks, lat, picked)
    sent[...] = dot(picked[...], dflat[...]).astype(bf16)
    lat_term[...] = dot(weight[...], dflat[...], TRANS_B).astype(bf16)


def keep_kernel(depth, blocks, lat, dflat, other, keep_k, keep_v, send_k, send_v, picked):
    pick_blocks(depth, blocks, lat, picked)
    half, cols = keep_k.shape
    for at, send, keep in ((0, send_k, keep_k), (cols, send_v, keep_v)):
        part = slice(at, at + cols)
        send[...] = (dot(picked[half:], dflat[:, part]) + other[half:, part].astype(f32)).astype(bf16)
        keep[...] = dot(picked[:half], dflat[:, part]) + other[:half, part].astype(f32)


def sum_kernel(parts, after, out):
    total = parts[0].astype(f32)
    for i in range(1, parts.shape[0]):
        total += parts[i].astype(f32)
    out[...] = total.astype(bf16)


def call(kernel, specs, shapes, scratch, flops, *args):
    size = sum(a.size * a.dtype.itemsize for a in args)
    return pl.pallas_call(
        kernel,
        out_shape=shapes,
        in_specs=specs,
        out_specs=jax.tree.map(lambda _: VMEM, shapes),
        scratch_shapes=scratch,
        compiler_params=pltpu.CompilerParams(vmem_limit_bytes=16 << 20),
        cost_estimate=pl.CostEstimate(flops=flops, bytes_accessed=size, transcendentals=0),
    )(*args)


def body(queries, latents, kv_weight, token_image, image_counts, out_grad):
    samples, keys, depth = latents.shape
    rows = samples * keys
    _, width, _, local = kv_weight.shape
    weight = kv_weight.reshape(width, 2 * local)
    core = lax.axis_index("core")
    lat = gather_latents(latents.reshape(rows, depth).T)

    half, cols = width // 4, 2 * local
    zs = jnp.stack(relative("zh"))

    def blocks(at_core, ys):
        return (zs[None, :] * 8 + jnp.stack(ys)[:, None] * 2 + at_core).reshape(-1).astype(jnp.int32)

    mine, second, first, both = relative("y")
    picked = pltpu.VMEM((2 * half, rows), bf16)
    attended, dflat, grad_send, lat_term = call(
        functools.partial(main_kernel, keys, depth),
        [SMEM] * 2 + [VMEM] * 5,
        (
            jax.ShapeDtypeStruct(queries.shape[1:], bf16),
            jax.ShapeDtypeStruct((rows, cols), bf16),
            jax.ShapeDtypeStruct((2 * half, cols), bf16),
            jax.ShapeDtypeStruct((width, rows), bf16),
        ),
        [pltpu.VMEM((rows, cols), bf16), picked],
        5 * rows * width * cols,
        image_counts,
        blocks(1 - core, [mine, first, second, both]),
        lat,
        weight,
        queries[0],
        out_grad[0],
        token_image.reshape(samples, 1, -1),
    )
    keep_k, keep_v, send_k, send_v = call(
        functools.partial(keep_kernel, depth),
        [SMEM, VMEM, VMEM, VMEM],
        (jax.ShapeDtypeStruct((half, local), f32),) * 2 + (jax.ShapeDtypeStruct((half, local), bf16),) * 2,
        [picked],
        width * rows * cols,
        blocks(core, [mine, second, first, both]),
        lat,
        dflat,
        swap(grad_send, "core", 1),
    )

    lat_parts = lax.all_to_all(lat_term.reshape(4, half, rows), "section", 0, 0, tiled=True)
    lat_sum = call(
        sum_kernel,
        [VMEM, pl.BlockSpec(memory_space=pl.ANY)],
        jax.ShapeDtypeStruct((half, rows), bf16),
        [],
        4 * half * rows,
        lat_parts,
        send_v,
    )
    lat_parts = lax.all_to_all(lat_sum.reshape(8, depth, rows), "mp", 0, 0, tiled=True)

    lat_sum = jnp.sum(lat_parts.astype(f32), axis=0)

    def split(x):
        return x.reshape(2, -1, local)

    key = split(keep_k + paired(send_k, "y", True).astype(f32))
    value = split(keep_v + paired(send_v, "y", True).astype(f32))
    key = split(key[0] + paired(key[1].astype(bf16), "y", False).astype(f32))
    value = split(value[0] + paired(value[1].astype(bf16), "y", False).astype(f32))
    key = split(key[0] + paired(key[1].astype(bf16), "zh", True).astype(f32))
    value = split(value[0] + paired(value[1].astype(bf16), "zh", True).astype(f32))
    value, lat_sum = lax.optimization_barrier((value, lat_sum))
    key = key[0] + paired(key[1].astype(bf16), "zh", False).astype(f32)
    value = value[0] + paired(value[1].astype(bf16), "zh", False).astype(f32)
    kv_grad = jnp.stack([key, value], axis=1)
    return (
        attended[None],
        kv_grad.reshape(1, depth, 2, local),
        lat_sum.T.reshape(samples, keys, depth),
    )


def solution(mesh):
    fine = Mesh(mesh.devices.reshape([n for _, n in SIZES]), AXES)
    return jax.shard_map(
        body,
        mesh=fine,
        in_specs=(
            P("section", DP, None, "mp"),
            P(DP, None, ("section", "mp")),
            P("section", None, None, "mp"),
            P(DP, None),
            P(DP),
            P("section", DP, None, "mp"),
        ),
        out_specs=(
            P("section", DP, None, "mp"),
            P("section", DP, None, "mp"),
            P(DP, None, ("section", "mp")),
        ),
        check_vma=False,
    )
```

```python
import functools

import jax
import jax.numpy as jnp
from jax import lax
from jax.experimental import pallas as pl
from jax.experimental.pallas import tpu as pltpu
from jax.sharding import Mesh, PartitionSpec as P

HEAD = 128
LATENTS = 64
SIZES = (("zh", 4), ("y", 4), ("core", 2), ("section", 4), ("mp", 8))
AXES = tuple(name for name, _ in SIZES)
SIZE = dict(SIZES)
DP = ("zh", "y", "core")
f32, bf16 = jnp.float32, jnp.bfloat16
VMEM = pl.BlockSpec(memory_space=pltpu.VMEM)
SMEM = pl.BlockSpec(memory_space=pltpu.SMEM)
TRANS_A = (((0,), (0,)), ((), ()))
TRANS_B = (((1,), (1,)), ((), ()))


def dot(a, b, dims=(((1,), (0,)), ((), ()))):
    return lax.dot_general(a, b, dims, preferred_element_type=f32)


PARITY = {"y": "core", "section": "core", "zh": "mp"}


def relative(axis):
    me, odd = lax.axis_index(axis), lax.axis_index(PARITY[axis]) % 2
    return [me, me ^ (3 - 2 * odd), me ^ (1 + 2 * odd), me ^ 2]


def paired(x, axis, first):
    axes = tuple(name for name in AXES if name in (axis, PARITY[axis]))
    pairs = []
    for at in range(SIZE[axes[0]] * SIZE[axes[1]]):
        place = dict(zip(axes, divmod(at, SIZE[axes[1]])))
        odd = place[PARITY[axis]] % 2
        place[axis] ^= 1 + 2 * odd if first else 3 - 2 * odd
        pairs.append((at, place[axes[0]] * SIZE[axes[1]] + place[axes[1]]))
    return lax.ppermute(x, axes, pairs)


def swap(x, axis, bit):
    return lax.ppermute(x, axis, [(i, i ^ bit) for i in range(SIZE[axis])])


def gather_latents(own):
    block = own
    for axis in ("mp", "section"):
        copies = jnp.broadcast_to(block, (SIZE[axis],) + block.shape)
        block = lax.all_to_all(copies, axis, 0, 0, tiled=True)
        block = block.reshape((-1,) + block.shape[2:])
    return block


def pick_blocks(depth, blocks, lat, picked):
    for i in range(picked.shape[0] // depth):
        start = pl.multiple_of(blocks[i] * depth, 16)
        picked[i * depth : (i + 1) * depth, :] = lat[pl.ds(start, depth), :]


def main_kernel(
    keys, depth, counts, blocks, lat, weight, query, grad, token, attended, dflat, sent, lat_term, kv, picked
):
    samples, _, width = query.shape
    scale = HEAD ** (-0.5)
    kv[...] = dot(lat[...], weight[...], TRANS_A).astype(bf16)
    image_of = lax.broadcasted_iota(jnp.int32, (keys, query.shape[1]), 0) // LATENTS
    for b in range(samples):
        rows = slice(b * keys, (b + 1) * keys)
        allowed = (image_of == token[b]) & (image_of < counts[b])
        for h in range(width // HEAD):
            low = slice(h * HEAD, (h + 1) * HEAD)
            high = slice(width + h * HEAD, width + (h + 1) * HEAD)
            k, v, q, g = kv[rows, low], kv[rows, high], query[b, :, low], grad[b, :, low]
            scores = dot(k, q, TRANS_B) * scale
            top = jnp.max(jnp.where(allowed, scores, -1e30), axis=0, keepdims=True)
            expval = jnp.where(allowed, jnp.exp(scores - top), 0.0)
            total = jnp.sum(expval, axis=0, keepdims=True)
            prob = expval / jnp.where(total > 0, total, 1.0)
            prob_bf = prob.astype(bf16)
            attended[b, :, low] = dot(prob_bf, v, TRANS_A).astype(bf16)
            dprob = dot(v, g, TRANS_B)
            dscore = prob * (dprob - jnp.sum(dprob * prob, axis=0, keepdims=True)) * scale
            dflat[rows, low] = dot(dscore.astype(bf16), q).astype(bf16)
            dflat[rows, high] = dot(prob_bf, g).astype(bf16)
    pick_blocks(depth, blocks, lat, picked)
    sent[...] = dot(picked[...], dflat[...]).astype(bf16)
    lat_term[...] = dot(weight[...], dflat[...], TRANS_B).astype(bf16)


def keep_kernel(depth, blocks, lat, dflat, other, keep_k, keep_v, send_k, send_v, picked):
    pick_blocks(depth, blocks, lat, picked)
    half, cols = keep_k.shape
    for at, send, keep in ((0, send_k, keep_k), (cols, send_v, keep_v)):
        part = slice(at, at + cols)
        send[...] = (dot(picked[half:], dflat[:, part]) + other[half:, part].astype(f32)).astype(bf16)
        keep[...] = dot(picked[:half], dflat[:, part]) + other[:half, part].astype(f32)


def sum_kernel(depth, place, parts, after, out):
    total = parts[0].astype(f32)
    for i in range(1, parts.shape[0]):
        total += parts[i].astype(f32)
    for m in range(out.shape[0] // depth):
        at = pl.multiple_of(place[m] * depth, 16)
        out[pl.ds(at, depth), :] = total[m * depth : (m + 1) * depth]


def call(kernel, specs, shapes, scratch, flops, *args):
    size = sum(a.size * a.dtype.itemsize for a in args)
    return pl.pallas_call(
        kernel,
        out_shape=shapes,
        in_specs=specs,
        out_specs=jax.tree.map(lambda _: VMEM, shapes),
        scratch_shapes=scratch,
        compiler_params=pltpu.CompilerParams(vmem_limit_bytes=16 << 20),
        cost_estimate=pl.CostEstimate(flops=flops, bytes_accessed=size, transcendentals=0),
    )(*args)


def body(queries, latents, kv_weight, token_image, image_counts, out_grad):
    samples, keys, depth = latents.shape
    rows = samples * keys
    _, width, _, local = kv_weight.shape
    weight = kv_weight.reshape(width, 2 * local)
    core = lax.axis_index("core")
    lat = gather_latents(latents.reshape(rows, depth).T)

    half, cols = width // 4, 2 * local
    zs = jnp.stack(relative("zh"))

    def blocks(at_core, ys):
        return (zs[None, :] * 8 + jnp.stack(ys)[:, None] * 2 + at_core).reshape(-1).astype(jnp.int32)

    mine, second, first, both = relative("y")
    picked = pltpu.VMEM((2 * half, rows), bf16)
    attended, dflat, grad_send, lat_term = call(
        functools.partial(main_kernel, keys, depth),
        [SMEM] * 2 + [VMEM] * 5,
        (
            jax.ShapeDtypeStruct(queries.shape[1:], bf16),
            jax.ShapeDtypeStruct((rows, cols), bf16),
            jax.ShapeDtypeStruct((2 * half, cols), bf16),
            jax.ShapeDtypeStruct((width, rows), bf16),
        ),
        [pltpu.VMEM((rows, cols), bf16), picked],
        5 * rows * width * cols,
        image_counts,
        blocks(1 - core, [mine, first, second, both]),
        lat,
        weight,
        queries[0],
        out_grad[0],
        token_image.reshape(samples, 1, -1),
    )
    keep_k, keep_v, send_k, send_v = call(
        functools.partial(keep_kernel, depth),
        [SMEM, VMEM, VMEM, VMEM],
        (jax.ShapeDtypeStruct((half, local), f32),) * 2 + (jax.ShapeDtypeStruct((half, local), bf16),) * 2,
        [picked],
        width * rows * cols,
        blocks(core, [mine, second, first, both]),
        lat,
        dflat,
        swap(grad_send, "core", 1),
    )

    def split(x):
        return x.reshape(2, -1, local)

    lat_parts = lax.all_to_all(lat_term.reshape(4, half, rows), "section", 0, 0, tiled=True)
    key = split(keep_k + paired(send_k, "y", True).astype(f32))
    value = split(keep_v + paired(send_v, "y", True).astype(f32))
    last = value[1].astype(bf16)
    grad = jnp.concatenate(
        [
            key[0] + paired(key[1].astype(bf16), "y", False).astype(f32),
            value[0] + paired(last, "y", False).astype(f32),
        ],
        axis=-1,
    ).reshape(2, -1, cols)
    send = grad[1].astype(bf16)

    to = jnp.arange(8, dtype=jnp.int32) ^ lax.axis_index("mp")
    lat_sum = call(
        functools.partial(sum_kernel, depth),
        [SMEM, VMEM, pl.BlockSpec(memory_space=pl.ANY)],
        jax.ShapeDtypeStruct((half, rows), f32),
        [],
        4 * half * rows,
        (to % 2) * 4 + (to // 2 % 2) * 2 + to // 4,
        lat_parts,
        last,
    ).reshape(8, depth, rows)
    lat_sum = lat_sum[:4] + swap(lat_sum[4:].astype(bf16), "mp", 1).astype(f32)

    lat_send = lat_sum[2:].astype(bf16)
    send, lat_send = lax.optimization_barrier((send, lat_send))

    grad = (grad[0] + paired(send, "zh", True).astype(f32)).reshape(2, -1, cols)
    kv_grad = grad[0] + paired(grad[1].astype(bf16), "zh", False).astype(f32)
    lat_sum = lat_sum[:2] + swap(lat_send, "mp", 2).astype(f32)
    lat_sum = lat_sum[0] + swap(lat_sum[1].astype(bf16), "mp", 4).astype(f32)
    return (
        attended[None],
        kv_grad.reshape(1, depth, 2, local),
        lat_sum.T.reshape(samples, keys, depth),
    )


def solution(mesh):
    fine = Mesh(mesh.devices.reshape([n for _, n in SIZES]), AXES)
    return jax.shard_map(
        body,
        mesh=fine,
        in_specs=(
            P("section", DP, None, "mp"),
            P(DP, None, ("section", "mp")),
            P("section", None, None, "mp"),
            P(DP, None),
            P(DP),
            P("section", DP, None, "mp"),
        ),
        out_specs=(
            P("section", DP, None, "mp"),
            P("section", DP, None, "mp"),
            P(DP, None, ("section", "mp")),
        ),
        check_vma=False,
    )
```

```python
import functools

import jax
import jax.numpy as jnp
from jax import lax
from jax.experimental import pallas as pl
from jax.experimental.pallas import tpu as pltpu
from jax.sharding import Mesh, PartitionSpec as P

HEAD = 128
LATENTS = 64
SIZES = (("zh", 4), ("y", 4), ("core", 2), ("section", 4), ("mp", 8))
AXES = tuple(name for name, _ in SIZES)
SIZE = dict(SIZES)
DP = ("zh", "y", "core")
f32, bf16 = jnp.float32, jnp.bfloat16
VMEM = pl.BlockSpec(memory_space=pltpu.VMEM)
SMEM = pl.BlockSpec(memory_space=pltpu.SMEM)
TRANS_A = (((0,), (0,)), ((), ()))
TRANS_B = (((1,), (1,)), ((), ()))


def dot(a, b, dims=(((1,), (0,)), ((), ()))):
    return lax.dot_general(a, b, dims, preferred_element_type=f32)


PARITY = {"y": "core", "section": "core", "zh": "mp"}


def relative(axis):
    me, odd = lax.axis_index(axis), lax.axis_index(PARITY[axis]) % 2
    return [me, me ^ (3 - 2 * odd), me ^ (1 + 2 * odd), me ^ 2]


def paired(x, axis, first):
    axes = tuple(name for name in AXES if name in (axis, PARITY[axis]))
    pairs = []
    for at in range(SIZE[axes[0]] * SIZE[axes[1]]):
        place = dict(zip(axes, divmod(at, SIZE[axes[1]])))
        odd = place[PARITY[axis]] % 2
        place[axis] ^= 1 + 2 * odd if first else 3 - 2 * odd
        pairs.append((at, place[axes[0]] * SIZE[axes[1]] + place[axes[1]]))
    return lax.ppermute(x, axes, pairs)


def swap(x, axis, bit):
    return lax.ppermute(x, axis, [(i, i ^ bit) for i in range(SIZE[axis])])


def gather_latents(own):
    block = own
    for axis in ("mp", "section"):
        copies = jnp.broadcast_to(block, (SIZE[axis],) + block.shape)
        block = lax.all_to_all(copies, axis, 0, 0, tiled=True)
        block = block.reshape((-1,) + block.shape[2:])
    return block


def pick_blocks(depth, blocks, lat, picked):
    for i in range(picked.shape[0] // depth):
        start = pl.multiple_of(blocks[i] * depth, 16)
        picked[i * depth : (i + 1) * depth, :] = lat[pl.ds(start, depth), :]


def main_kernel(
    keys, depth, counts, blocks, lat, weight, query, grad, token, attended, dflat, sent, lat_term, kv, picked
):
    samples, _, width = query.shape
    scale = HEAD ** (-0.5)
    kv[...] = dot(lat[...], weight[...], TRANS_A).astype(bf16)
    image_of = lax.broadcasted_iota(jnp.int32, (keys, query.shape[1]), 0) // LATENTS
    for b in range(samples):
        rows = slice(b * keys, (b + 1) * keys)
        allowed = (image_of == token[b]) & (image_of < counts[b])
        for h in range(width // HEAD):
            low = slice(h * HEAD, (h + 1) * HEAD)
            high = slice(width + h * HEAD, width + (h + 1) * HEAD)
            k, v, q, g = kv[rows, low], kv[rows, high], query[b, :, low], grad[b, :, low]
            scores = dot(k, q, TRANS_B) * scale
            top = jnp.max(jnp.where(allowed, scores, -1e30), axis=0, keepdims=True)
            expval = jnp.where(allowed, jnp.exp(scores - top), 0.0)
            total = jnp.sum(expval, axis=0, keepdims=True)
            prob = expval / jnp.where(total > 0, total, 1.0)
            prob_bf = prob.astype(bf16)
            attended[b, :, low] = dot(prob_bf, v, TRANS_A).astype(bf16)
            dprob = dot(v, g, TRANS_B)
            dscore = prob * (dprob - jnp.sum(dprob * prob, axis=0, keepdims=True)) * scale
            dflat[rows, low] = dot(dscore.astype(bf16), q).astype(bf16)
            dflat[rows, high] = dot(prob_bf, g).astype(bf16)
    pick_blocks(depth, blocks, lat, picked)
    sent[...] = dot(picked[...], dflat[...]).astype(bf16)
    lat_term[...] = dot(weight[...], dflat[...], TRANS_B).astype(bf16)


def keep_kernel(depth, blocks, lat, dflat, other, keep, send, picked):
    pick_blocks(depth, blocks, lat, picked)
    half, cols = keep.shape[0], keep.shape[1] // 2
    for at in (0, cols):
        part = slice(at, at + cols)
        send[:, part] = (dot(picked[half:], dflat[:, part]) + other[half:, part].astype(f32)).astype(bf16)
        keep[:, part] = dot(picked[:half], dflat[:, part]) + other[:half, part].astype(f32)


def sum_kernel(depth, place, parts, out):
    total = parts[0].astype(f32)
    for i in range(1, parts.shape[0]):
        total += parts[i].astype(f32)
    for m in range(out.shape[0] // depth):
        at = pl.multiple_of(place[m] * depth, 16)
        out[pl.ds(at, depth), :] = total[m * depth : (m + 1) * depth]


def call(kernel, specs, shapes, scratch, flops, *args):
    size = sum(a.size * a.dtype.itemsize for a in args)
    return pl.pallas_call(
        kernel,
        out_shape=shapes,
        in_specs=specs,
        out_specs=jax.tree.map(lambda _: VMEM, shapes),
        scratch_shapes=scratch,
        compiler_params=pltpu.CompilerParams(vmem_limit_bytes=16 << 20),
        cost_estimate=pl.CostEstimate(flops=flops, bytes_accessed=size, transcendentals=0),
    )(*args)


def body(queries, latents, kv_weight, token_image, image_counts, out_grad):
    samples, keys, depth = latents.shape
    rows = samples * keys
    _, width, _, local = kv_weight.shape
    weight = kv_weight.reshape(width, 2 * local)
    core = lax.axis_index("core")
    lat = gather_latents(latents.reshape(rows, depth).T)

    half, cols = width // 4, 2 * local
    zs = jnp.stack(relative("zh"))

    def blocks(at_core, ys):
        return (zs[None, :] * 8 + jnp.stack(ys)[:, None] * 2 + at_core).reshape(-1).astype(jnp.int32)

    mine, second, first, both = relative("y")
    picked = pltpu.VMEM((2 * half, rows), bf16)
    attended, dflat, grad_send, lat_term = call(
        functools.partial(main_kernel, keys, depth),
        [SMEM] * 2 + [VMEM] * 5,
        (
            jax.ShapeDtypeStruct(queries.shape[1:], bf16),
            jax.ShapeDtypeStruct((rows, cols), bf16),
            jax.ShapeDtypeStruct((2 * half, cols), bf16),
            jax.ShapeDtypeStruct((width, rows), bf16),
        ),
        [pltpu.VMEM((rows, cols), bf16), picked],
        5 * rows * width * cols,
        image_counts,
        blocks(1 - core, [mine, first, second, both]),
        lat,
        weight,
        queries[0],
        out_grad[0],
        token_image.reshape(samples, 1, -1),
    )
    keep, send = call(
        functools.partial(keep_kernel, depth),
        [SMEM, VMEM, VMEM, VMEM],
        (jax.ShapeDtypeStruct((half, cols), f32), jax.ShapeDtypeStruct((half, cols), bf16)),
        [picked],
        width * rows * cols,
        blocks(core, [mine, second, first, both]),
        lat,
        dflat,
        swap(grad_send, "core", 1),
    )

    lat_parts = lax.all_to_all(lat_term.reshape(4, half, rows), "section", 0, 0, tiled=True)
    grad = (keep + paired(send, "y", True).astype(f32)).reshape(2, -1, cols)
    last = grad[1].astype(bf16)
    grad = (grad[0] + paired(last, "y", False).astype(f32)).reshape(2, -1, cols)
    send = grad[1].astype(bf16)

    to = jnp.arange(8, dtype=jnp.int32) ^ lax.axis_index("mp")
    lat_sum = call(
        functools.partial(sum_kernel, depth),
        [SMEM, VMEM],
        jax.ShapeDtypeStruct((half, rows), f32),
        [],
        4 * half * rows,
        (to % 2) * 4 + (to // 2 % 2) * 2 + to // 4,
        lat_parts,
    ).reshape(8, depth, rows)
    lat_sum = lat_sum[:4] + swap(lat_sum[4:].astype(bf16), "mp", 1).astype(f32)

    grad = (grad[0] + paired(send, "zh", True).astype(f32)).reshape(2, -1, cols)
    lat_sum = lat_sum[:2] + swap(lat_sum[2:].astype(bf16), "mp", 2).astype(f32)
    last = lat_sum[1].astype(bf16)
    send, last = lax.optimization_barrier((grad[1].astype(bf16), last))
    kv_grad = grad[0] + paired(send, "zh", False).astype(f32)
    lat_sum = lat_sum[0] + swap(last, "mp", 4).astype(f32)
    return (
        attended[None],
        kv_grad.reshape(1, depth, 2, local),
        lat_sum.T.reshape(samples, keys, depth),
    )


def solution(mesh):
    fine = Mesh(mesh.devices.reshape([n for _, n in SIZES]), AXES)
    return jax.shard_map(
        body,
        mesh=fine,
        in_specs=(
            P("section", DP, None, "mp"),
            P(DP, None, ("section", "mp")),
            P("section", None, None, "mp"),
            P(DP, None),
            P(DP),
            P("section", DP, None, "mp"),
        ),
        out_specs=(
            P("section", DP, None, "mp"),
            P("section", DP, None, "mp"),
            P(DP, None, ("section", "mp")),
        ),
        check_vma=False,
    )
```

```python
import functools

import jax
import jax.numpy as jnp
from jax import lax
from jax.experimental import pallas as pl
from jax.experimental.pallas import tpu as pltpu
from jax.sharding import Mesh, PartitionSpec as P

HEAD = 128
LATENTS = 64
SIZES = (("zh", 4), ("y", 4), ("core", 2), ("section", 4), ("mp", 8))
AXES = tuple(name for name, _ in SIZES)
SIZE = dict(SIZES)
DP = ("zh", "y", "core")
f32, bf16 = jnp.float32, jnp.bfloat16
VMEM = pl.BlockSpec(memory_space=pltpu.VMEM)
SMEM = pl.BlockSpec(memory_space=pltpu.SMEM)
TRANS_A = (((0,), (0,)), ((), ()))
TRANS_B = (((1,), (1,)), ((), ()))


def dot(a, b, dims=(((1,), (0,)), ((), ()))):
    return lax.dot_general(a, b, dims, preferred_element_type=f32)


PARITY = {"y": "core", "section": "core", "zh": "core"}


def relative(axis):
    me, odd = lax.axis_index(axis), lax.axis_index(PARITY[axis]) % 2
    return [me, me ^ (3 - 2 * odd), me ^ (1 + 2 * odd), me ^ 2]


def paired(x, axis, first):
    axes = tuple(name for name in AXES if name in (axis, PARITY[axis]))
    pairs = []
    for at in range(SIZE[axes[0]] * SIZE[axes[1]]):
        place = dict(zip(axes, divmod(at, SIZE[axes[1]])))
        odd = place[PARITY[axis]] % 2
        place[axis] ^= 1 + 2 * odd if first else 3 - 2 * odd
        pairs.append((at, place[axes[0]] * SIZE[axes[1]] + place[axes[1]]))
    return lax.ppermute(x, axes, pairs)


def swap(x, axis, bit):
    return lax.ppermute(x, axis, [(i, i ^ bit) for i in range(SIZE[axis])])


def gather_latents(own):
    block = own
    for axis in ("mp", "section"):
        copies = jnp.broadcast_to(block, (SIZE[axis],) + block.shape)
        block = lax.all_to_all(copies, axis, 0, 0, tiled=True)
        block = block.reshape((-1,) + block.shape[2:])
    return block


def pick_blocks(depth, blocks, lat, picked):
    for i in range(picked.shape[0] // depth):
        start = pl.multiple_of(blocks[i] * depth, 16)
        picked[i * depth : (i + 1) * depth, :] = lat[pl.ds(start, depth), :]


def main_kernel(
    keys, depth, counts, blocks, lat, weight, query, grad, token, attended, dflat, sent, lat_term, kv, picked
):
    samples, _, width = query.shape
    scale = HEAD ** (-0.5)
    kv[...] = dot(lat[...], weight[...], TRANS_A).astype(bf16)
    image_of = lax.broadcasted_iota(jnp.int32, (keys, query.shape[1]), 0) // LATENTS
    for b in range(samples):
        rows = slice(b * keys, (b + 1) * keys)
        allowed = (image_of == token[b]) & (image_of < counts[b])
        for h in range(width // HEAD):
            low = slice(h * HEAD, (h + 1) * HEAD)
            high = slice(width + h * HEAD, width + (h + 1) * HEAD)
            k, v, q, g = kv[rows, low], kv[rows, high], query[b, :, low], grad[b, :, low]
            scores = dot(k, q, TRANS_B) * scale
            top = jnp.max(jnp.where(allowed, scores, -1e30), axis=0, keepdims=True)
            expval = jnp.where(allowed, jnp.exp(scores - top), 0.0)
            total = jnp.sum(expval, axis=0, keepdims=True)
            prob = expval / jnp.where(total > 0, total, 1.0)
            prob_bf = prob.astype(bf16)
            attended[b, :, low] = dot(prob_bf, v, TRANS_A).astype(bf16)
            dprob = dot(v, g, TRANS_B)
            dscore = prob * (dprob - jnp.sum(dprob * prob, axis=0, keepdims=True)) * scale
            dflat[rows, low] = dot(dscore.astype(bf16), q).astype(bf16)
            dflat[rows, high] = dot(prob_bf, g).astype(bf16)
    pick_blocks(depth, blocks, lat, picked)
    sent[...] = dot(picked[...], dflat[...]).astype(bf16)
    lat_term[...] = dot(weight[...], dflat[...], TRANS_B).astype(bf16)


def keep_kernel(depth, blocks, lat, dflat, other, keep, send, picked):
    pick_blocks(depth, blocks, lat, picked)
    half, cols = keep.shape[0], keep.shape[1] // 2
    for at in (0, cols):
        part = slice(at, at + cols)
        send[:, part] = (dot(picked[half:], dflat[:, part]) + other[half:, part].astype(f32)).astype(bf16)
        keep[:, part] = dot(picked[:half], dflat[:, part]) + other[:half, part].astype(f32)


def sum_kernel(depth, place, parts, out):
    total = parts[0].astype(f32)
    for i in range(1, parts.shape[0]):
        total += parts[i].astype(f32)
    for m in range(out.shape[0] // depth):
        at = pl.multiple_of(place[m] * depth, 16)
        out[pl.ds(at, depth), :] = total[m * depth : (m + 1) * depth]


def call(kernel, specs, shapes, scratch, flops, *args):
    size = sum(a.size * a.dtype.itemsize for a in args)
    return pl.pallas_call(
        kernel,
        out_shape=shapes,
        in_specs=specs,
        out_specs=jax.tree.map(lambda _: VMEM, shapes),
        scratch_shapes=scratch,
        compiler_params=pltpu.CompilerParams(vmem_limit_bytes=16 << 20),
        cost_estimate=pl.CostEstimate(flops=flops, bytes_accessed=size, transcendentals=0),
    )(*args)


def body(queries, latents, kv_weight, token_image, image_counts, out_grad):
    samples, keys, depth = latents.shape
    rows = samples * keys
    _, width, _, local = kv_weight.shape
    weight = kv_weight.reshape(width, 2 * local)
    core = lax.axis_index("core")
    lat = gather_latents(latents.reshape(rows, depth).T)

    half, cols = width // 4, 2 * local

    def blocks(at_core, zs, ys):
        zs, ys = jnp.stack(zs), jnp.stack(ys)
        return (zs[None, :] * 8 + ys[:, None] * 2 + at_core).reshape(-1).astype(jnp.int32)

    own_order = relative("zh"), relative("y")
    other_order = [[mine, first, second, both] for mine, second, first, both in own_order]
    picked = pltpu.VMEM((2 * half, rows), bf16)
    attended, dflat, grad_send, lat_term = call(
        functools.partial(main_kernel, keys, depth),
        [SMEM] * 2 + [VMEM] * 5,
        (
            jax.ShapeDtypeStruct(queries.shape[1:], bf16),
            jax.ShapeDtypeStruct((rows, cols), bf16),
            jax.ShapeDtypeStruct((2 * half, cols), bf16),
            jax.ShapeDtypeStruct((width, rows), bf16),
        ),
        [pltpu.VMEM((rows, cols), bf16), picked],
        5 * rows * width * cols,
        image_counts,
        blocks(1 - core, *other_order),
        lat,
        weight,
        queries[0],
        out_grad[0],
        token_image.reshape(samples, 1, -1),
    )
    keep, send = call(
        functools.partial(keep_kernel, depth),
        [SMEM, VMEM, VMEM, VMEM],
        (jax.ShapeDtypeStruct((half, cols), f32), jax.ShapeDtypeStruct((half, cols), bf16)),
        [picked],
        width * rows * cols,
        blocks(core, *own_order),
        lat,
        dflat,
        swap(grad_send, "core", 1),
    )

    lat_parts = lax.all_to_all(lat_term.reshape(4, half, rows), "section", 0, 0, tiled=True)
    grad = (keep + paired(send, "y", True).astype(f32)).reshape(2, -1, cols)
    last = grad[1].astype(bf16)
    grad = (grad[0] + paired(last, "y", False).astype(f32)).reshape(2, -1, cols)
    send = grad[1].astype(bf16)

    to = jnp.arange(8, dtype=jnp.int32) ^ lax.axis_index("mp")
    lat_sum = call(
        functools.partial(sum_kernel, depth),
        [SMEM, VMEM],
        jax.ShapeDtypeStruct((half, rows), f32),
        [],
        4 * half * rows,
        (to % 2) * 4 + (to // 2 % 2) * 2 + to // 4,
        lat_parts,
    ).reshape(8, depth, rows)
    lat_sum = lat_sum[:4] + swap(lat_sum[4:].astype(bf16), "mp", 1).astype(f32)

    grad = (grad[0] + paired(send, "zh", True).astype(f32)).reshape(2, -1, cols)
    lat_sum = lat_sum[:2] + swap(lat_sum[2:].astype(bf16), "mp", 2).astype(f32)
    last = lat_sum[1].astype(bf16)
    send, last = lax.optimization_barrier((grad[1].astype(bf16), last))
    kv_grad = grad[0] + paired(send, "zh", False).astype(f32)
    lat_sum = lat_sum[0] + swap(last, "mp", 4).astype(f32)
    return (
        attended[None],
        kv_grad.reshape(1, depth, 2, local),
        lat_sum.T.reshape(samples, keys, depth),
    )


def solution(mesh):
    fine = Mesh(mesh.devices.reshape([n for _, n in SIZES]), AXES)
    return jax.shard_map(
        body,
        mesh=fine,
        in_specs=(
            P("section", DP, None, "mp"),
            P(DP, None, ("section", "mp")),
            P("section", None, None, "mp"),
            P(DP, None),
            P(DP),
            P("section", DP, None, "mp"),
        ),
        out_specs=(
            P("section", DP, None, "mp"),
            P("section", DP, None, "mp"),
            P(DP, None, ("section", "mp")),
        ),
        check_vma=False,
    )
```

```python
import functools

import jax
import jax.numpy as jnp
from jax import lax
from jax.experimental import pallas as pl
from jax.experimental.pallas import tpu as pltpu
from jax.sharding import Mesh, PartitionSpec as P

HEAD = 128
LATENTS = 64
SIZES = (("zh", 4), ("y", 4), ("core", 2), ("section", 4), ("mp", 8))
AXES = tuple(name for name, _ in SIZES)
SIZE = dict(SIZES)
DP = ("zh", "y", "core")
f32, bf16 = jnp.float32, jnp.bfloat16
VMEM = pl.BlockSpec(memory_space=pltpu.VMEM)
SMEM = pl.BlockSpec(memory_space=pltpu.SMEM)
TRANS_A = (((0,), (0,)), ((), ()))
TRANS_B = (((1,), (1,)), ((), ()))


def dot(a, b, dims=(((1,), (0,)), ((), ()))):
    return lax.dot_general(a, b, dims, preferred_element_type=f32)


PARITY = {"y": "core", "section": "core", "zh": "core"}


def relative(axis):
    me, odd = lax.axis_index(axis), lax.axis_index(PARITY[axis]) % 2
    return [me, me ^ (3 - 2 * odd), me ^ (1 + 2 * odd), me ^ 2]


def paired(x, axis, first):
    axes = tuple(name for name in AXES if name in (axis, PARITY[axis]))
    pairs = []
    for at in range(SIZE[axes[0]] * SIZE[axes[1]]):
        place = dict(zip(axes, divmod(at, SIZE[axes[1]])))
        odd = place[PARITY[axis]] % 2
        place[axis] ^= 1 + 2 * odd if first else 3 - 2 * odd
        pairs.append((at, place[axes[0]] * SIZE[axes[1]] + place[axes[1]]))
    return lax.ppermute(x, axes, pairs)


def swap(x, axis, bit):
    return lax.ppermute(x, axis, [(i, i ^ bit) for i in range(SIZE[axis])])


def gather_latents(own):
    block = own
    for axis in ("mp", "section"):
        copies = jnp.broadcast_to(block, (SIZE[axis],) + block.shape)
        block = lax.all_to_all(copies, axis, 0, 0, tiled=True)
        block = block.reshape((-1,) + block.shape[2:])
    return block


def pick_blocks(depth, blocks, lat, picked):
    for i in range(picked.shape[0] // depth):
        start = pl.multiple_of(blocks[i] * depth, 16)
        picked[i * depth : (i + 1) * depth, :] = lat[pl.ds(start, depth), :]


def main_kernel(
    keys, depth, counts, blocks, lat, weight, query, grad, token, attended, dflat, sent, lat_term, kv, picked
):
    samples, _, width = query.shape
    scale = HEAD ** (-0.5)
    kv[...] = dot(lat[...], weight[...], TRANS_A).astype(bf16)
    image_of = lax.broadcasted_iota(jnp.int32, (keys, query.shape[1]), 0) // LATENTS
    for b in range(samples):
        rows = slice(b * keys, (b + 1) * keys)
        allowed = (image_of == token[b]) & (image_of < counts[b])
        for h in range(width // HEAD):
            low = slice(h * HEAD, (h + 1) * HEAD)
            high = slice(width + h * HEAD, width + (h + 1) * HEAD)
            k, v, q, g = kv[rows, low], kv[rows, high], query[b, :, low], grad[b, :, low]
            scores = dot(k, q, TRANS_B) * scale
            top = jnp.max(jnp.where(allowed, scores, -1e30), axis=0, keepdims=True)
            expval = jnp.where(allowed, jnp.exp(scores - top), 0.0)
            total = jnp.sum(expval, axis=0, keepdims=True)
            prob = expval / jnp.where(total > 0, total, 1.0)
            prob_bf = prob.astype(bf16)
            attended[b, :, low] = dot(prob_bf, v, TRANS_A).astype(bf16)
            dprob = dot(v, g, TRANS_B)
            dscore = prob * (dprob - jnp.sum(dprob * prob, axis=0, keepdims=True)) * scale
            dflat[rows, low] = dot(dscore.astype(bf16), q).astype(bf16)
            dflat[rows, high] = dot(prob_bf, g).astype(bf16)
    pick_blocks(depth, blocks, lat, picked)
    sent[...] = dot(picked[...], dflat[...]).astype(bf16)
    lat_term[...] = dot(weight[...], dflat[...], TRANS_B).astype(bf16)


def keep_kernel(depth, blocks, lat, dflat, other, keep, send, picked):
    pick_blocks(depth, blocks, lat, picked)
    half, cols = keep.shape[0], keep.shape[1] // 2
    for at in (0, cols):
        part = slice(at, at + cols)
        send[:, part] = (dot(picked[half:], dflat[:, part]) + other[half:, part].astype(f32)).astype(bf16)
        keep[:, part] = dot(picked[:half], dflat[:, part]) + other[:half, part].astype(f32)


def sum_kernel(depth, place, parts, out):
    total = parts[0].astype(f32)
    for i in range(1, parts.shape[0]):
        total += parts[i].astype(f32)
    for m in range(out.shape[0] // depth):
        at = pl.multiple_of(place[m] * depth, 16)
        out[pl.ds(at, depth), :] = total[m * depth : (m + 1) * depth]


def call(kernel, specs, shapes, scratch, flops, *args):
    size = sum(a.size * a.dtype.itemsize for a in args)
    return pl.pallas_call(
        kernel,
        out_shape=shapes,
        in_specs=specs,
        out_specs=jax.tree.map(lambda _: VMEM, shapes),
        scratch_shapes=scratch,
        compiler_params=pltpu.CompilerParams(vmem_limit_bytes=16 << 20),
        cost_estimate=pl.CostEstimate(flops=flops, bytes_accessed=size, transcendentals=0),
    )(*args)


def body(queries, latents, kv_weight, token_image, image_counts, out_grad):
    samples, keys, depth = latents.shape
    rows = samples * keys
    _, width, _, local = kv_weight.shape
    weight = kv_weight.reshape(width, 2 * local)
    core = lax.axis_index("core")
    lat = gather_latents(latents.reshape(rows, depth).T)

    half, cols = width // 4, 2 * local

    def blocks(at_core, zs, ys):
        zs, ys = jnp.stack(zs), jnp.stack(ys)
        return (zs[None, :] * 8 + ys[:, None] * 2 + at_core).reshape(-1).astype(jnp.int32)

    own_order = relative("zh"), relative("y")
    other_order = [[mine, first, second, both] for mine, second, first, both in own_order]
    picked = pltpu.VMEM((2 * half, rows), bf16)
    attended, dflat, grad_send, lat_term = call(
        functools.partial(main_kernel, keys, depth),
        [SMEM] * 2 + [VMEM] * 5,
        (
            jax.ShapeDtypeStruct(queries.shape[1:], bf16),
            jax.ShapeDtypeStruct((rows, cols), bf16),
            jax.ShapeDtypeStruct((2 * half, cols), bf16),
            jax.ShapeDtypeStruct((width, rows), bf16),
        ),
        [pltpu.VMEM((rows, cols), bf16), picked],
        5 * rows * width * cols,
        image_counts,
        blocks(1 - core, *other_order),
        lat,
        weight,
        queries[0],
        out_grad[0],
        token_image.reshape(samples, 1, -1),
    )
    keep, send = call(
        functools.partial(keep_kernel, depth),
        [SMEM, VMEM, VMEM, VMEM],
        (jax.ShapeDtypeStruct((half, cols), f32), jax.ShapeDtypeStruct((half, cols), bf16)),
        [picked],
        width * rows * cols,
        blocks(core, *own_order),
        lat,
        dflat,
        swap(grad_send, "core", 1),
    )

    lat_parts = lax.all_to_all(lat_term.reshape(4, half, rows), "section", 0, 0, tiled=True)
    grad = (keep + paired(send, "y", True).astype(f32)).reshape(2, -1, cols)
    last = grad[1].astype(bf16)
    grad = (grad[0] + paired(last, "y", False).astype(f32)).reshape(2, -1, cols)
    send = grad[1].astype(bf16)

    to = jnp.arange(8, dtype=jnp.int32) ^ lax.axis_index("mp")
    lat_sum = call(
        functools.partial(sum_kernel, depth),
        [SMEM, VMEM],
        jax.ShapeDtypeStruct((half, rows), f32),
        [],
        4 * half * rows,
        (to % 2) * 4 + (to // 2 % 2) * 2 + to // 4,
        lat_parts,
    ).reshape(8, depth, rows)
    lat_sum = lat_sum[:4] + swap(lat_sum[4:].astype(bf16), "mp", 1).astype(f32)

    grad = (grad[0] + paired(send, "zh", True).astype(f32)).reshape(2, -1, cols)
    lat_sum = lat_sum[:2] + swap(lat_sum[2:].astype(bf16), "mp", 2).astype(f32)
    kv_grad = grad[0] + paired(grad[1].astype(bf16), "zh", False).astype(f32)
    lat_sum = lat_sum[0] + swap(lat_sum[1].astype(bf16), "mp", 4).astype(f32)
    return (
        attended[None],
        kv_grad.reshape(1, depth, 2, local),
        lat_sum.T.reshape(samples, keys, depth),
    )


def solution(mesh):
    fine = Mesh(mesh.devices.reshape([n for _, n in SIZES]), AXES)
    return jax.shard_map(
        body,
        mesh=fine,
        in_specs=(
            P("section", DP, None, "mp"),
            P(DP, None, ("section", "mp")),
            P("section", None, None, "mp"),
            P(DP, None),
            P(DP),
            P("section", DP, None, "mp"),
        ),
        out_specs=(
            P("section", DP, None, "mp"),
            P("section", DP, None, "mp"),
            P(DP, None, ("section", "mp")),
        ),
        check_vma=False,
    )
```
